256 devices in a mesh: eng: 32 (over y_hi, z, core), exp: 8 (over y_lo, x).
Axes of the slice: x: 4, y: 4 (y_hi: 2, y_lo: 2; y = y_hi * 2 + y_lo), z: 8, core: 2. Of those that a mesh axis runs over, the one named last changes fastest.
Arguments:
- residual_in: bfloat16 [4096, 4096], P(('eng', 'exp')), may hold values from -6 to 6
- queries: bfloat16 [2, 4096, 4096], P(None, ('eng', 'exp')), may hold values from -256 to 256
- kv_cache: bfloat16 [4096, 16, 2, 512], P(('eng', 'exp')), may hold values from -5 to 5
- new_kv: bfloat16 [2, 4096, 2, 512], P(None, ('eng', 'exp')), may hold values from -5 to 5
- lengths: int32 [4096], P(('eng', 'exp')), may hold values from 2 to 16, as said below
- out_weight: bfloat16 [4096, 4096], P('exp'), may hold values from -0.09375 to 0.09375
- norm_gain: float32 [4096], replicated, may hold values from 0.5 to 1.5
- sectioned_gate_up: bfloat16 [32, 8, 4096, 384], P('eng', 'exp'), may hold values from -0.09375 to 0.09375
- sectioned_down: bfloat16 [32, 8, 192, 4096], P('eng', 'exp'), may hold values from -0.21875 to 0.21875
- owners: int32 [32], replicated, may hold values from 0 to 31, each once
- expert_ids: int32 [2, 4096, 1], P(None, ('eng', 'exp')), may hold values from 0 to 7; in each aligned block of 16 rows (0 to 15, 16 to 31, ..., all dimensions but the last counted through in order) at most 4 rows name the same one
- route_weight: float32 [2, 4096], P(None, ('eng', 'exp')), may hold values from 0.2 to 1
Outputs:
- updated: bfloat16 [4096, 4096], P(('eng', 'exp'))
The draws below stay inside these ranges and needn't reach their ends.
Inputs may be any that keep to these rules, and one draw needn't show every extreme that they name: Each engine index once; block b comes from owners[b] for b < 4. `expert_ids`: in each step at most 4 of the 16 rows of one device name one expert. `lengths`: one row of every device has 16.
All inputs are finite; a program needn't handle non-finite values.
Results may differ from the reference program's by a relative error of at most 0.015.
Values may be sent and summed in bfloat16 or wider, within the bound.
No kernel may reach another device: no remote copies, remote signals or barrier semaphores. Data moves between devices by JAX's collectives and lax.ppermute only.
A program may use at most 128 MiB of HBM per device.

```python
import math
import jax
import jax.numpy as jnp
import numpy as np
from jax import lax

D = 4096
FF = 768
BLOCKS = 4
HQ = 32
KVH = 4
HD = 128
L = 16
ROWS_DEV = 16
BH = 192
EXPERTS = 8
CAP = 4
TOKENS = 4096
N_ENG = 32
N_EXP = 8


def shared_cache(key):
    return jnp.clip(jax.random.normal(key, (TOKENS, L, 2, KVH * HD), jnp.float32), -5.0, 5.0)


def draw_kv_cache(key, part):
    drawn = shared_cache(key)
    return drawn.astype(jnp.bfloat16)


def draw_queries(key, part):
    key = jax.random.fold_in(key, 2)
    result = jnp.clip(jax.random.normal(key, (2, TOKENS, HQ * HD), jnp.float32), -5.0, 5.0)
    return result.astype(jnp.bfloat16)


def draw_lengths(key, part):
    key = jax.random.fold_in(key, 3)
    drawn = jax.random.randint(key, (TOKENS,), 2, L + 1)
    row_index = jnp.arange(TOKENS)
    return jnp.where(row_index % ROWS_DEV == 0, L, drawn).astype(jnp.int32)


def level_of(stream_key, dims, split, least, high):
    level, own = 1.0, jax.random.fold_in(stream_key, 6)
    for dim, blocks in split:
        heights = jnp.exp(jax.random.uniform(jax.random.fold_in(own, dim), (blocks,), jnp.float32, least / len(split), high / len(split)))
        level = level * jnp.repeat(heights, dims[dim] // blocks).reshape([-1 if axis == dim else 1 for axis in range(len(dims))])
    return level


def shared_out(rng, own, number, rows, count, top, bound, slope):
    ranking = jax.random.permutation(rng, count)
    packed, usual = load_shares(count, rows * top, bound, slope, True), load_shares(count, rows * top, bound, slope, False)
    places = jnp.arange(count)

    def named(sizes, turn):
        used = int((sizes > 0).sum())
        fixed = max(1, used // 4)
        moved = fixed + (places - fixed + turn * (used - fixed)) % max(1, count - fixed)
        return jnp.zeros((count,), jnp.int32).at[ranking[jnp.where(places < fixed, places, moved)]].set(jnp.asarray(sizes, jnp.int32))

    sizes = jnp.where(number % 4 == 0, named(packed, number // 4), named(usual, number - number // 4 - 1))
    mixed = jax.random.permutation(jax.random.fold_in(own, 3), count)
    donor, taker = mixed[0:count // 2 * 2:2], mixed[1:count // 2 * 2:2]
    slack = jnp.minimum(sizes[donor] - 1, bound - sizes[taker]) // 2
    slack = jnp.where((donor == ranking[0]) | (taker == ranking[0]) | (sizes[taker] == 0), 0, jnp.maximum(slack, 0))
    moved = jax.random.randint(jax.random.fold_in(own, 4), (count // 2,), 0, 1 << 20) % (slack + 1)
    sizes = sizes.at[donor].add(-moved).at[taker].add(moved)
    items = jnp.searchsorted(jnp.cumsum(sizes), jnp.arange(rows * top), side="right").astype(jnp.int32)
    table = items.reshape(top, rows).T
    table = table[jax.random.permutation(jax.random.fold_in(own, 1), rows)]
    turn = jax.random.randint(jax.random.fold_in(own, 2), (rows, 1), 0, top)
    return jnp.take_along_axis(table, (jnp.arange(top)[None, :] + turn) % top, axis=1)


def load_shares(count, total, most, slope, full):
    portions = [(1 << 20) // math.isqrt(standing ** slope) + 1 for standing in range(1, count + 1)]
    largest = most if full else min(most, max(-(-total // count), total * portions[0] // sum(portions)))
    least = 1 if total - largest >= count - 1 else 0
    holding, rest = [largest] + [least] * (count - 1), total - largest - least * (count - 1)
    while rest > 0:
        free = [i for i in range(1, count) if holding[i] < largest] or [i for i in range(1, count) if holding[i] < most]
        mass, left = sum([portions[i] for i in free]), rest
        for i in free:
            more = min(most - holding[i], max(1, left * portions[i] // mass), rest)
            holding[i] = holding[i] + more
            rest = rest - more
    return np.array(holding)


def normal_values(rng, shape, spread, bound, pieces=(), kind=jnp.bfloat16):
    values = spread * jax.random.normal(rng, shape, jnp.float32)
    if pieces:
        values = values * level_of(rng, shape, pieces, -0.22, 0.18)
    return jnp.clip(values, -bound, bound).astype(kind)


def setup_inputs(seed: int = 0) -> dict:
    splits = jax.random.split(jax.random.key(seed), 13)
    residual_in = normal_values(splits[0], (TOKENS, D), 1.0, 6.0, ((0, 256),))
    queries = draw_queries(jax.random.fold_in(splits[12], 71), 0)
    kv_cache = draw_kv_cache(jax.random.fold_in(splits[12], 71), 0)
    new_kv = normal_values(splits[3], (2, TOKENS, 2, KVH * HD), 1.0, 5.0, ((1, 256),))
    lengths = draw_lengths(jax.random.fold_in(splits[12], 71), 0)
    out_weight = normal_values(splits[5], (HQ * HD, D), (HQ * HD) ** -0.5, 0.09375, ((0, 8),))
    norm_gain = jnp.clip(1.0 + 0.1 * jax.random.normal(splits[6], (D,), jnp.float32), 0.5, 1.5)
    sectioned_gate_up = normal_values(splits[7], (N_ENG, EXPERTS, D, 2 * BH), D ** -0.5, 0.09375, ((0, 32), (1, 8)))
    sectioned_down = normal_values(splits[8], (N_ENG, EXPERTS, BH, D), FF ** -0.5, 0.21875, ((0, 32), (1, 8)))
    owners = jax.random.permutation(splits[9], N_ENG).astype(jnp.int32)
    expert_ids_keys = jax.random.split(jax.random.fold_in(splits[10], 1), 2 * TOKENS // ROWS_DEV)
    expert_ids_turns = jax.random.permutation(jax.random.fold_in(splits[10], 3), 2 * TOKENS // ROWS_DEV)
    expert_ids = jax.vmap(lambda own, number: shared_out(jax.random.fold_in(splits[10], 2), own, number, ROWS_DEV, EXPERTS, 1, CAP, 2))(expert_ids_keys, expert_ids_turns).reshape((2, TOKENS, 1))
    route_weight = jnp.clip(jnp.exp(math.log(1.0) - 1.609438 * jax.random.uniform(splits[11], (2, TOKENS), jnp.float32) ** level_of(splits[11], (2, TOKENS), ((1, 256),), -0.2, 0.2)), 0.2, 1.0)
    return {"residual_in": residual_in, "queries": queries, "kv_cache": kv_cache, "new_kv": new_kv, "lengths": lengths, "out_weight": out_weight, "norm_gain": norm_gain, "sectioned_gate_up": sectioned_gate_up, "sectioned_down": sectioned_down, "owners": owners, "expert_ids": expert_ids, "route_weight": route_weight}


def attend(queries, key_rows, value_rows, visible):
    row_count = queries.shape[0]
    places = key_rows.shape[1]
    query_heads = queries.astype(jnp.float32).reshape(row_count, KVH, HQ // KVH, HD)
    key_heads = key_rows.astype(jnp.float32).reshape(row_count, places, KVH, HD)
    value_heads = value_rows.astype(jnp.float32).reshape(row_count, places, KVH, HD)
    scores = jnp.einsum('rkgd,rpkd->rkgp', query_heads, key_heads) * (1.0 / math.sqrt(HD))
    scores = jnp.where(visible[:, None, None, :], scores, jnp.float32(-1e+30))
    row_max = lax.optimization_barrier(jnp.max(scores, axis=-1, keepdims=True))
    weights = jnp.exp(scores - row_max)
    probability = (weights / lax.optimization_barrier(jnp.sum(weights, axis=-1, keepdims=True))).astype(jnp.bfloat16)
    mixed = jnp.einsum('rkgp,rpkd->rkgd', probability.astype(jnp.float32), value_heads)
    return mixed.reshape(row_count, HQ * HD).astype(jnp.bfloat16)

def expert_rows(inputs, gate_up, down):
    half_width = down.shape[1]
    summed = jnp.zeros((inputs.shape[0], down.shape[2]), jnp.float32)
    for block_index in range(gate_up.shape[0]):
        gate_up_out = jnp.dot(inputs, gate_up[block_index], preferred_element_type=jnp.float32)
        hidden = (jax.nn.silu(gate_up_out[:, :half_width]) * gate_up_out[:, half_width:]).astype(jnp.bfloat16)
        summed = summed + jnp.dot(hidden, down[block_index], preferred_element_type=jnp.float32)
    return summed.astype(jnp.bfloat16)

def reference(residual_in, queries, kv_cache, new_kv, lengths, out_weight, norm_gain, sectioned_gate_up, sectioned_down, owners, expert_ids, route_weight):
    gate_up = jnp.stack([sectioned_gate_up[owners[b]] for b in range(BLOCKS)], axis=1)
    down = jnp.stack([sectioned_down[owners[b]] for b in range(BLOCKS)], axis=1)
    hidden_state = residual_in.astype(jnp.float32)
    tokens = residual_in.shape[0]
    places = L + 2
    position = jnp.arange(places, dtype=jnp.int32)
    group_width = HQ * HD // N_EXP
    nblock = tokens // ROWS_DEV
    capacity = 2 * ROWS_DEV // N_EXP
    for decode_step in range(2):
        key_rows = jnp.concatenate([kv_cache[:, :, 0], jnp.transpose(new_kv[:, :, 0], (1, 0, 2))], axis=1)
        value_rows = jnp.concatenate([kv_cache[:, :, 1], jnp.transpose(new_kv[:, :, 1], (1, 0, 2))], axis=1)
        visible = (position[None, :] < lengths[:, None]) | (position[None, :] >= L) & (position[None, :] <= L + decode_step)
        attended = attend(queries[decode_step], key_rows, value_rows, visible)
        projected = jnp.zeros((tokens, D), jnp.float32)
        for g in range(N_EXP):
            partial_value = jnp.dot(attended[:, g * group_width:(g + 1) * group_width], out_weight[g * group_width:(g + 1) * group_width], preferred_element_type=jnp.float32).astype(jnp.bfloat16)
            partial_value = lax.optimization_barrier(partial_value)
            projected = projected + partial_value.astype(jnp.float32)
        hidden_state = hidden_state + projected
        normed = (hidden_state * lax.rsqrt(lax.optimization_barrier(jnp.mean(hidden_state * hidden_state, axis=-1, keepdims=True)) + 1e-06) * norm_gain).astype(jnp.bfloat16)
        chosen = expert_ids[decode_step, :, 0].astype(jnp.int32)
        onehot = (chosen[:, None] == jnp.arange(N_EXP, dtype=jnp.int32)[None, :]).astype(jnp.int32).reshape(nblock, ROWS_DEV, N_EXP)
        before = jnp.cumsum(onehot, axis=1) - onehot
        slot_rank = lax.optimization_barrier(jnp.sum(before * onehot, axis=-1)).reshape(tokens).astype(jnp.int32)
        slot_index = jnp.arange(tokens, dtype=jnp.int32) // ROWS_DEV * capacity + slot_rank
        buffer = jnp.zeros((N_EXP, nblock * capacity, D), jnp.bfloat16).at[chosen, slot_index].set(normed)
        results = lax.map(lambda expert_item: expert_rows(expert_item[0], expert_item[1], expert_item[2]), (buffer, gate_up, down))
        returned = results[chosen, slot_index]
        hidden_state = hidden_state + route_weight[decode_step][:, None] * returned.astype(jnp.float32)
    return hidden_state.astype(jnp.bfloat16)
```

```python
import math

import jax
import jax.numpy as jnp
from jax import lax
from jax.experimental import pallas as pl
from jax.experimental.pallas import tpu as pltpu
from jax.sharding import Mesh
from jax.sharding import PartitionSpec as P

BLOCKS = 4
HQ = 32
KVH = 4
HD = 128
NZ = 8
ROWS = 16
CAP = 4
EXPERTS = 8
PLACES = 16
D = 4096
BH = 192
QH = BH // 4
CHUNK = D // NZ
ENG = ("yh", "z", "c")
EXP = ("yl", "x")
PLANE = ("yh", "yl", "x")
EVERY = ENG + EXP


def pack_kernel(core_ref, gate_up_ref, down_ref, keep_ref, give_ref):
    turned = jnp.transpose(gate_up_ref[...])
    down = down_ref[...]

    def put(out_ref, core):
        for plane in range(2):
            h = (plane * 2 + core) * QH
            out_ref[0, plane, 0:QH, :] = turned[h : h + QH]
            out_ref[0, plane, QH : 2 * QH, :] = turned[BH + h : BH + h + QH]
            out_ref[0, plane, 2 * QH : 3 * QH, :] = down[h : h + QH]

    @pl.when(core_ref[0] == 0)
    def _():
        put(keep_ref, 0)
        put(give_ref, 1)

    @pl.when(core_ref[0] == 1)
    def _():
        put(keep_ref, 1)
        put(give_ref, 0)


def pack(core, gate_up, down):
    shape = jax.ShapeDtypeStruct((NZ, 2, 3 * QH, CHUNK), jnp.bfloat16)
    out_spec = pl.BlockSpec((1, 2, 3 * QH, CHUNK), lambda i, core_ref: (i, 0, 0, 0))
    return pl.pallas_call(
        pack_kernel,
        out_shape=(shape, shape),
        grid_spec=pltpu.PrefetchScalarGridSpec(
            num_scalar_prefetch=1,
            grid=(NZ,),
            in_specs=[
                pl.BlockSpec((CHUNK, 2 * BH), lambda i, core_ref: (i, 0)),
                pl.BlockSpec((BH, CHUNK), lambda i, core_ref: (0, i)),
            ],
            out_specs=[out_spec, out_spec],
        ),
        compiler_params=pltpu.CompilerParams(vmem_limit_bytes=16 * 1024 * 1024),
        cost_estimate=pl.CostEstimate(flops=0, bytes_accessed=9 * 2**20, transcendentals=0),
        name="pack_slot",
    )(core, gate_up, down)


def attend_kernel(q_ref, kv_ref, new_ref, cached_bias_ref, new_bias_ref, out_ref):
    group = HQ // KVH
    cached_bias = jnp.concatenate([cached_bias_ref[...]] * group, axis=0)
    new_bias = jnp.concatenate([new_bias_ref[...]] * group, axis=0)
    nt = (((1,), (1,)), ((), ()))
    rows = 2 * ROWS
    for k in range(KVH):
        q = jnp.concatenate(
            [q_ref[:, (k * group + g) * HD : (k * group + g + 1) * HD] for g in range(group)],
            axis=0,
        )
        key_c = kv_ref[:, k * HD : (k + 1) * HD]
        val_c = kv_ref[:, (KVH + k) * HD : (KVH + k + 1) * HD]
        key_n = new_ref[:, k * HD : (k + 1) * HD]
        val_n = new_ref[:, (KVH + k) * HD : (KVH + k + 1) * HD]
        scale = 1.0 / math.sqrt(HD)
        s_c = lax.dot_general(q, key_c, nt, preferred_element_type=jnp.float32) * scale
        s_n = lax.dot_general(q, key_n, nt, preferred_element_type=jnp.float32) * scale
        s_c = jnp.where(cached_bias > 0.0, s_c, -1e30)
        s_n = jnp.where(new_bias > 0.0, s_n, -1e30)
        top = jnp.maximum(
            jnp.max(s_c, axis=1, keepdims=True), jnp.max(s_n, axis=1, keepdims=True)
        )
        w_c = jnp.exp(s_c - top)
        w_n = jnp.exp(s_n - top)
        total = jnp.sum(w_c, axis=1, keepdims=True) + jnp.sum(w_n, axis=1, keepdims=True)
        p_c = (w_c / total).astype(jnp.bfloat16)
        p_n = (w_n / total).astype(jnp.bfloat16)
        mixed = jnp.dot(p_c, val_c, preferred_element_type=jnp.float32) + jnp.dot(
            p_n, val_n, preferred_element_type=jnp.float32
        )
        mixed = mixed.astype(jnp.bfloat16)
        for g in range(group):
            head = k * group + g
            lane = (head % 4) * HD
            out_ref[head // 4, :, lane : lane + HD] = mixed[g * rows : (g + 1) * rows]


def attend(q, kv, new, cached_seen, new_seen):
    return pl.pallas_call(
        attend_kernel,
        out_shape=jax.ShapeDtypeStruct((EXPERTS, 2 * ROWS, D // EXPERTS), jnp.bfloat16),
        compiler_params=pltpu.CompilerParams(vmem_limit_bytes=16 * 1024 * 1024),
        cost_estimate=pl.CostEstimate(
            flops=2 * 2 * KVH * 256 * 288 * HD, bytes_accessed=2**20, transcendentals=KVH * 256 * 288
        ),
        name="attend_rows",
    )(q, kv, new, cached_seen, new_seen)


def expert_kernel(own_ref, other_ref, w_ref, own_out_ref, other_out_ref):
    rows = own_ref.shape[0]
    nt = (((1,), (1,)), ((), ()))
    x = jnp.concatenate([own_ref[...], other_ref[...]], axis=0)
    width = BLOCKS * QH
    acc = jnp.zeros((2 * rows, 2 * width), jnp.float32)
    for z in range(NZ):
        acc = acc + lax.dot_general(
            x[:, z * CHUNK : (z + 1) * CHUNK],
            w_ref[z, 0 : 2 * width, :],
            nt,
            preferred_element_type=jnp.float32,
        )
    gate = acc[:, :width]
    hidden = (gate / (1.0 + jnp.exp(-gate)) * acc[:, width:]).astype(jnp.bfloat16)
    for z in range(NZ):
        out = jnp.dot(
            hidden, w_ref[z, 2 * width : 3 * width, :], preferred_element_type=jnp.float32
        ).astype(jnp.bfloat16)
        own_out_ref[:, z * CHUNK : (z + 1) * CHUNK] = out[:rows]
        other_out_ref[:, z * CHUNK : (z + 1) * CHUNK] = out[rows:]


def expert(own, other, weights):
    shape = jax.ShapeDtypeStruct(own.shape, jnp.bfloat16)
    return pl.pallas_call(
        expert_kernel,
        out_shape=(shape, shape),
        compiler_params=pltpu.CompilerParams(vmem_limit_bytes=24 * 1024 * 1024),
        cost_estimate=pl.CostEstimate(
            flops=2 * 128 * 576 * D, bytes_accessed=7 * 2**20, transcendentals=128 * 192
        ),
        name="expert_rows",
    )(own, other, weights)


def swap(x, axis):
    return lax.ppermute(x, axis, [(0, 1), (1, 0)])


def refresh(gate_up, down, owners):
    yh, z, c = lax.axis_index("yh"), lax.axis_index("z"), lax.axis_index("c")
    owner = owners[:BLOCKS]
    owner_y, owner_z, owner_c = owner // (2 * NZ), owner // 2 % NZ, owner % 2
    keep, give = pack(c.reshape(1).astype(jnp.int32), gate_up, down)
    got = swap(give, "c")
    first_core = (yh * NZ + z) * 2
    first_wanted = jnp.any(owner == first_core)
    chosen = jnp.where(first_wanted, 0, 1)

    def scattered(core):
        sent = jnp.where(core == c, keep, got)
        return lax.all_to_all(sent, "z", split_axis=0, concat_axis=0, tiled=True)

    arrived = scattered(chosen)

    def pick(source, b, plane):
        return lax.dynamic_slice(
            source, (owner_z[b], plane, 0, 0), (1, 1, 3 * QH, CHUNK)
        ).reshape(3 * QH, CHUNK)

    mine = jnp.stack([pick(arrived, b, yh) for b in range(BLOCKS)])
    theirs = jnp.stack([pick(arrived, b, 1 - yh) for b in range(BLOCKS)])
    late = jnp.any((owner[:, None] == owner[None, :] + 1) & (owner[None, :] % 2 == 0), axis=1)

    def second(mine, theirs):
        again = scattered(jnp.int32(1))
        return tuple(
            jnp.stack(
                [jnp.where(late[b], pick(again, b, plane), first[b]) for b in range(BLOCKS)]
            )
            for first, plane in ((mine, yh), (theirs, 1 - yh))
        )

    mine, theirs = lax.cond(jnp.any(late), second, lambda a, b: (a, b), mine, theirs)
    crossed = swap(theirs, "yh")
    share = jnp.where((owner_y == yh)[:, None, None], mine, crossed)
    share = jnp.transpose(share.reshape(BLOCKS, 3, QH, CHUNK), (1, 0, 2, 3))
    share = share.reshape(1, 3 * BLOCKS * QH, CHUNK)
    return lax.all_gather(share, "z", axis=0, tiled=True)


def shards(
    residual_in,
    queries,
    kv_cache,
    new_kv,
    lengths,
    out_weight,
    norm_gain,
    sectioned_gate_up,
    sectioned_down,
    owners,
    expert_ids,
    route_weight,
):
    weights = refresh(sectioned_gate_up[0, 0], sectioned_down[0, 0], owners)

    row = jnp.arange(ROWS, dtype=jnp.int32)
    place = jnp.arange(PLACES, dtype=jnp.int32)
    step = jnp.arange(2, dtype=jnp.int32)
    same = row[:, None] == row[None, :]
    cached_seen = same[:, :, None] & (place[None, None, :] < lengths[:, None, None])
    cached_seen = jnp.broadcast_to(
        cached_seen.reshape(1, ROWS, ROWS * PLACES), (2, ROWS, ROWS * PLACES)
    ).reshape(2 * ROWS, ROWS * PLACES)
    new_seen = (step[:, None] >= step[None, :])[:, None, :, None] & same[None, :, None, :]
    new_seen = new_seen.reshape(2 * ROWS, 2 * ROWS)
    attended = attend(
        queries.reshape(2 * ROWS, D),
        kv_cache.reshape(ROWS * PLACES, 2 * KVH * HD),
        new_kv.reshape(2 * ROWS, 2 * KVH * HD),
        cached_seen.astype(jnp.float32),
        new_seen.astype(jnp.float32),
    )
    grouped = lax.all_to_all(attended, EXP, split_axis=0, concat_axis=0, tiled=True)
    partial = jnp.dot(
        grouped.reshape(EXPERTS * 2 * ROWS, D // EXPERTS),
        out_weight,
        preferred_element_type=jnp.float32,
    ).astype(jnp.bfloat16)
    partial = lax.all_to_all(
        partial.reshape(EXPERTS, 2 * ROWS, D), EXP, split_axis=0, concat_axis=0, tiled=True
    )
    projected = jnp.sum(partial.astype(jnp.float32), axis=0).reshape(2, ROWS, D)

    hidden_state = residual_in.astype(jnp.float32)
    for decode_step in range(2):
        hidden_state = hidden_state + projected[decode_step]
        normed = (
            hidden_state
            * lax.rsqrt(jnp.mean(hidden_state * hidden_state, axis=-1, keepdims=True) + 1e-06)
            * norm_gain
        ).astype(jnp.bfloat16)
        chosen = expert_ids[decode_step, :, 0]
        onehot = (chosen[:, None] == jnp.arange(EXPERTS, dtype=jnp.int32)[None, :]).astype(
            jnp.int32
        )
        before = jnp.cumsum(onehot, axis=0) - onehot
        slot_index = chosen * CAP + jnp.sum(before * onehot, axis=1)
        selector = (
            slot_index[:, None] == jnp.arange(EXPERTS * CAP, dtype=jnp.int32)[None, :]
        ).astype(jnp.bfloat16)
        selector = jnp.concatenate([selector, selector], axis=1)
        outgoing = jnp.dot(selector.T, normed, preferred_element_type=jnp.float32).astype(
            jnp.bfloat16
        )
        own = lax.all_to_all(
            outgoing.reshape(2 * EXPERTS, CAP, D), PLANE, split_axis=0, concat_axis=0, tiled=True
        ).reshape(2 * EXPERTS * CAP, D)
        own_out, other_out = expert(own, swap(own, "c"), weights)
        finished = (
            own_out.astype(jnp.float32) + swap(other_out, "c").astype(jnp.float32)
        ).astype(jnp.bfloat16)
        returned = lax.all_to_all(
            finished.reshape(2 * EXPERTS, CAP, D), PLANE, split_axis=0, concat_axis=0, tiled=True
        ).reshape(2 * EXPERTS * CAP, D)
        collected = jnp.dot(selector, returned, preferred_element_type=jnp.float32)
        hidden_state = hidden_state + route_weight[decode_step][:, None] * collected
    return hidden_state.astype(jnp.bfloat16)


def solution(mesh):
    fine = Mesh(mesh.devices.reshape(2, NZ, 2, 2, 4), EVERY)
    return jax.shard_map(
        shards,
        mesh=fine,
        in_specs=(
            P(EVERY, None),
            P(None, EVERY, None),
            P(EVERY, None, None, None),
            P(None, EVERY, None, None),
            P(EVERY),
            P(EXP, None),
            P(),
            P(ENG, EXP, None, None),
            P(ENG, EXP, None, None),
            P(),
            P(None, EVERY, None),
            P(None, EVERY),
        ),
        out_specs=P(EVERY, None),
        check_vma=False,
    )
```
